32 devices in a mesh: groups: 2 (over y), acq: 8 (over z, x), rng: 2 (over core).
Axes of the slice: x: 2, y: 2, z: 4, core: 2. Of those that a mesh axis runs over, the one named last changes fastest.
Arguments:
- slc: bfloat16 [2, 16, 64, 2048], P(None, ('groups', 'acq'), None, 'rng'), parts along dimension 1, may hold values from -32 to 32, as said below
- map_cell: int32 [16, 256], P('groups', 'rng'), parts along dimension 0, may hold values from 0 to 16383, as said below
Outputs:
- geocoded: float32 [3, 8, 2, 16384], P(None, 'groups', None, ('acq', 'rng')), parts along dimension 1
The draws below stay inside these ranges and needn't reach their ends.
There are 2 independent parts, one for each index of `groups`. The reference program is written for one: setup_inputs(seed, part) draws one part's arguments, and reference() takes and returns one part's arrays. A program takes and returns all parts, laid end to end along the dimension named above; each array names one. Nothing has to cross between parts.
Inputs may be any that keep to these rules, and one draw needn't show every extreme that they name: `slc`: samples of an acquisition share a scene phase with the others, up to a per-sample phase drift. `map_cell`: A map cell is row * 128 + column on a grid of 128 rows; several radar cells may share one, and some map cells receive none. Nothing more is promised about where a radar cell lands.
All inputs are finite; a program needn't handle non-finite values.
Results may differ from the reference program's by a relative error of at most 0.0003.
Values may be sent and summed in bfloat16 or wider, within the bound.
A program may use at most 128 MiB of HBM per device.

```python
import math
import jax
import jax.numpy as jnp
from jax import lax

LINES = 64
LOOK_A = 8
LOOK_R = 8
HALF_W = 4
ROUNDS = 3
MAPC = 16384
MAPROW = 128
MAPCOL = 128
ACQ = 8
PAIRS = 4
NRNG = 2048
MLL = 8
MLR = 256


def draw_slc(key, part):
    key_list = jax.random.split(jax.random.fold_in(key, 11), 4)
    grid_shape = (ACQ, LINES, NRNG)
    amplitude = jnp.exp(jax.random.uniform(key_list[0], (1, LINES, NRNG), minval=0.0, maxval=math.log(10.0)))
    spread = 0.8
    jitter_terms = 0.4 * jnp.clip(jax.random.normal(key_list[3], (2,) + grid_shape), -4.0, 4.0)
    scene_phase = jax.random.uniform(key_list[1], (1, LINES, NRNG), minval=-math.pi, maxval=math.pi)
    drift_phase = spread * jax.random.normal(key_list[2], grid_shape)
    full_phase = scene_phase + drift_phase
    real_part = amplitude * (jnp.cos(full_phase) + jitter_terms[0])
    imag_part = amplitude * (jnp.sin(full_phase) + jitter_terms[1])
    return jnp.clip(jnp.stack([real_part, imag_part]), -32.0, 32.0).astype(jnp.bfloat16)


def draw_map_cell(key, part):
    key_list = jax.random.split(jax.random.fold_in(key, 23), 4)
    line_ids = jnp.arange(MLL, dtype=jnp.int32)[:, None]
    col_ids = jnp.arange(MLR, dtype=jnp.int32)[None, :]
    row_step = MAPROW // MLL
    coarse_rows = MLL // 4 + 1
    coarse_cols = MLR // 8 + 1
    terrain_col = jax.random.randint(key_list[0], (coarse_rows, coarse_cols), 0, 4, dtype=jnp.int32)
    terrain_row = jax.random.randint(key_list[1], (coarse_rows, coarse_cols), 0, 2, dtype=jnp.int32)
    coarse_line = jnp.broadcast_to(line_ids // 4, (MLL, MLR))
    coarse_col = jnp.broadcast_to(col_ids // 8, (MLL, MLR))
    shift_col = terrain_col[coarse_line, coarse_col]
    shift_row = terrain_row[coarse_line, coarse_col]
    fine_row = jax.random.randint(key_list[2], (MLL, MLR), 0, max(row_step, 1), dtype=jnp.int32)
    fine_col = jax.random.randint(key_list[3], (MLL, MLR), 0, 2, dtype=jnp.int32)
    map_row = jnp.clip(line_ids * MAPROW // MLL + fine_row + shift_row, 0, MAPROW - 1)
    map_col = jnp.clip(col_ids * MAPCOL // MLR + fine_col + shift_col - 2, 0, MAPCOL - 1)
    cells = (map_row * MAPCOL + map_col).astype(jnp.int32)
    cells = cells.at[0, 0].set(0)
    cells = cells.at[MLL - 1, MLR - 1].set(MAPC - 1)
    return cells


def setup_inputs(seed: int = 0, part: int = 0) -> dict:
    key_of = jax.random.split(jax.random.key(seed), 3)
    part_keys = jax.random.split(jax.random.fold_in(key_of[2], part), 3)
    slc = draw_slc(jax.random.fold_in(jax.random.fold_in(key_of[2], part), 71), part)
    map_cell = draw_map_cell(jax.random.fold_in(jax.random.fold_in(key_of[2], part), 71), part)
    return {"slc": slc, "map_cell": map_cell}


def look_sum(values_in):
    line_count, col_count = values_in.shape
    return values_in.reshape(line_count // LOOK_A, LOOK_A, col_count // LOOK_R, LOOK_R).sum(axis=(1, 3))

def smooth_range(values_in):
    rim_width = HALF_W
    col_count = values_in.shape[-1]
    padded = jnp.pad(values_in, [(0, 0)] * (values_in.ndim - 1) + [(rim_width, rim_width)])
    summed = jnp.zeros_like(values_in)
    for offset in range(-rim_width, rim_width + 1):
        weight = (rim_width + 1 - abs(offset)) / float((rim_width + 1) ** 2)
        summed = summed + weight * padded[..., rim_width + offset:rim_width + offset + col_count]
    return summed

def filter_pair(lower_slc, upper_slc):
    real_part = lower_slc[0] * upper_slc[0] + lower_slc[1] * upper_slc[1]
    imag_part = lower_slc[1] * upper_slc[0] - lower_slc[0] * upper_slc[1]
    power_low = look_sum(lower_slc[0] * lower_slc[0] + lower_slc[1] * lower_slc[1])
    power_up = look_sum(upper_slc[0] * upper_slc[0] + upper_slc[1] * upper_slc[1])
    inverse = 1.0 / jnp.sqrt(power_low * power_up + 1e-06)
    gamma = jnp.stack([look_sum(real_part) * inverse, look_sum(imag_part) * inverse])
    smooth = smooth_range(gamma)
    gain_term = (smooth[0] * smooth[0] + smooth[1] * smooth[1] + 0.01) ** (-0.25)
    return smooth * gain_term[None]

def reference(slc, map_cell):
    flat_cells = map_cell.reshape(-1).astype(jnp.int32)
    counts = jax.ops.segment_sum(jnp.ones(flat_cells.shape, jnp.float32), flat_cells, MAPC)
    divisor = jnp.maximum(counts, 1.0)
    results = []
    for round_index in range(ROUNDS):
        stride = 2 ** round_index
        pair_ids = jnp.arange(PAIRS, dtype=jnp.int32)
        lower_ids = pair_ids // stride * (2 * stride) + pair_ids % stride

        def one_pair(lower_index):
            lower_slc = lax.dynamic_index_in_dim(slc, lower_index, 1, keepdims=False).astype(jnp.float32)
            upper_slc = lax.dynamic_index_in_dim(slc, lower_index + stride, 1, keepdims=False).astype(jnp.float32)
            filtered = filter_pair(lower_slc, upper_slc)
            cell_sums = jnp.zeros((2, MAPC), jnp.float32).at[:, flat_cells].add(filtered.reshape(2, -1))
            return cell_sums / divisor[None]
        results.append(lax.map(one_pair, lower_ids))
    return jnp.stack(results)
```

```python
import functools

import jax
import jax.numpy as jnp
from jax import lax
from jax.experimental import pallas as pl
from jax.experimental.pallas import tpu as pltpu
from jax.sharding import PartitionSpec as P

LOOK_A = 8
LOOK_R = 8
HALF_W = 4
ROUNDS = 3
MAPC = 16384
BLOCK = 2**ROUNDS
PAIRS = BLOCK // 2
ROWS = ROUNDS * PAIRS * 2
MESH = pl.DeviceIdType.MESH
F32 = jnp.float32
BF16 = jnp.bfloat16


def split3(value):
    first = value.astype(BF16).astype(F32)
    rest = value - first
    second = rest.astype(BF16).astype(F32)
    return first, second, rest - second


def iota(shape, dim):
    return lax.broadcasted_iota(jnp.int32, shape, dim)


def kernel(
    acq_count,
    rng_count,
    slc_ref,
    map_ref,
    out_ref,
    samples,
    cells,
    gathered,
    one_hot,
    looks,
    band,
    own_sem,
    send_sem,
    recv_sem,
    map_send,
    map_recv,
    gather_send,
    gather_recv,
):
    group = acq_count * rng_count
    blocks = acq_count // BLOCK
    acq_rank = lax.axis_index("acq")
    rng_rank = lax.axis_index("rng")
    flat = acq_rank * rng_count + rng_rank
    base = acq_rank // BLOCK * BLOCK
    member = acq_rank % BLOCK
    tile_lines, tile_cols = samples.shape[2:]
    halves = slc_ref.shape[3] // tile_cols
    piece = out_ref.shape[2]

    def peer(step):
        other = (flat + step) % group
        return {"acq": other // rng_count, "rng": other % rng_count}, other

    def greet(step, carry):
        pl.semaphore_signal(barrier, inc=1, device_id=peer(step)[0], device_id_type=MESH)
        return carry

    barrier = pltpu.get_barrier_semaphore()
    lax.fori_loop(1, group, greet, 0)
    pl.semaphore_wait(barrier, group - 1)

    def tile_of(target):
        line = pl.multiple_of(target // halves * tile_lines, tile_lines)
        col = pl.multiple_of(target % halves * tile_cols, tile_cols)
        return slc_ref.at[:, 0, pl.ds(line, tile_lines), pl.ds(col, tile_cols)]

    sends = []
    for step in (4, 3, 5, 2, 6, 1, 7):
        target = (member + step) % BLOCK
        copy = pltpu.make_async_remote_copy(
            src_ref=tile_of(target),
            dst_ref=samples.at[member],
            send_sem=send_sem.at[step],
            recv_sem=recv_sem.at[member],
            device_id={"acq": base + target},
            device_id_type=MESH,
        )
        copy.start()
        sends.append(copy)
    own = pltpu.make_async_copy(tile_of(member), samples.at[member], own_sem)
    own.start()
    map_copy = pltpu.make_async_remote_copy(
        src_ref=map_ref,
        dst_ref=cells.at[rng_rank],
        send_sem=map_send,
        recv_sem=map_recv,
        device_id={"rng": 1 - rng_rank},
        device_id_type=MESH,
    )
    map_copy.start()
    cells[rng_rank] = map_ref[...]

    look_cells = tile_cols // LOOK_R
    lanes = looks.shape[1]
    looks[...] = jnp.where(
        iota(looks.shape, 0) // LOOK_R == iota(looks.shape, 1) % look_cells, 1.0, 0.0
    ).astype(BF16)
    source = iota(band.shape, 0)
    target = iota(band.shape, 1)
    wide = rng_count * halves * look_cells
    source_cell = source // lanes * look_cells + source % look_cells
    source_look = source % lanes // look_cells
    gap = jnp.abs(source_cell - target % wide)
    weight = jnp.where(source_look == target // wide, jnp.maximum(HALF_W + 1 - gap, 0), 0)
    band[...] = weight.astype(F32).astype(BF16)

    map_copy.wait()
    place = iota((piece, lanes), 0) + flat * piece
    for line in range(map_ref.shape[0]):
        for core in range(rng_count):
            row = cells[core, line : line + 1, :]
            one_hot[:, pl.ds((line * rng_count + core) * lanes, lanes)] = jnp.where(
                place == row, 1.0, 0.0
            ).astype(BF16)

    own.wait()
    for step in (1, 7, 2, 6, 3, 5, 4):
        origin = (member + step) % BLOCK
        pltpu.make_async_remote_copy(
            src_ref=samples.at[origin],
            dst_ref=samples.at[origin],
            send_sem=send_sem.at[step],
            recv_sem=recv_sem.at[origin],
            device_id={"acq": base + origin},
            device_id_type=MESH,
        ).wait_recv()

    real = [samples[a, 0].astype(F32) for a in range(BLOCK)]
    imag = [samples[a, 1].astype(F32) for a in range(BLOCK)]
    products = []
    pairs = []
    for r in range(ROUNDS):
        stride = 2**r
        for k in range(PAIRS):
            low = k // stride * 2 * stride + k % stride
            up = low + stride
            pairs.append((low, up))
            products.append(real[low] * real[up] + imag[low] * imag[up])
            products.append(imag[low] * real[up] - real[low] * imag[up])
    for a in range(BLOCK):
        products.append(real[a] * real[a] + imag[a] * imag[a])
    stacked = jnp.concatenate(products, axis=0)
    weights = looks[...]
    summed = sum(
        jnp.dot(part.astype(BF16), weights, preferred_element_type=F32)
        for part in reversed(split3(stacked))
    )
    summed = summed.reshape(len(products), tile_lines, lanes)
    lane = iota((1, 1, lanes), 2)
    chosen = jnp.where(lane < look_cells, summed[:, :LOOK_A], summed[:, LOOK_A:])
    sums = jnp.sum(chosen, axis=1)
    power = sums[ROWS:]
    power_low = jnp.concatenate([power[low : low + 1] for low, _ in pairs for _ in range(2)], axis=0)
    power_up = jnp.concatenate([power[up : up + 1] for _, up in pairs for _ in range(2)], axis=0)
    inverse = 1.0 / jnp.sqrt(power_low * power_up + 1e-06)
    gathered[flat] = sums[:ROWS] * inverse

    def gather_copy(step, index, slot):
        return pltpu.make_async_remote_copy(
            src_ref=gathered.at[slot],
            dst_ref=gathered.at[slot],
            send_sem=gather_send.at[step],
            recv_sem=gather_recv.at[slot],
            device_id=index,
            device_id_type=MESH,
        )

    def gather_start(step, carry):
        gather_copy(step, peer(step)[0], flat).start()
        return carry

    def gather_wait(step, carry):
        index, other = peer(step)
        gather_copy(step, index, other).wait_recv()
        return carry

    lax.fori_loop(1, group, gather_start, 0)
    for copy in sends:
        copy.wait_send()
    map_weights = one_hot[...]
    band_weights = band[...]
    lax.fori_loop(1, group, gather_wait, 0)

    quarters = BLOCK // halves
    even = iota((quarters * ROWS, 1), 0) % 2 == 0
    ones = jnp.ones((8, quarters * band.shape[1]), F32)

    def finish(block, carry):
        rows = []
        for q in range(quarters):
            parts = [
                gathered[(block * BLOCK + q * halves + h) * rng_count + c]
                for c in range(rng_count)
                for h in range(halves)
            ]
            rows.append(jnp.concatenate(parts, axis=1))
        gamma = jnp.concatenate(rows, axis=0)
        smooth = sum(
            jnp.dot(part.astype(BF16), band_weights, preferred_element_type=F32)
            for part in reversed(split3(gamma))
        ) * (1.0 / (HALF_W + 1) ** 2)
        square = smooth * smooth
        count = square.shape[0]
        partner = jnp.where(even, pltpu.roll(square, count - 1, 0), pltpu.roll(square, 1, 0))
        filtered = smooth * lax.rsqrt(jnp.sqrt(square + partner + 0.01))
        flat_rows = jnp.concatenate(
            [filtered[q * ROWS : (q + 1) * ROWS] for q in range(quarters)], axis=1
        )
        left = jnp.concatenate([*split3(flat_rows), ones], axis=0).astype(BF16)
        total = lax.dot_general(
            left, map_weights, (((1,), (1,)), ((), ())), preferred_element_type=F32
        )
        divisor = jnp.maximum(total[3 * ROWS : 3 * ROWS + 1], 1.0)
        result = (total[2 * ROWS : 3 * ROWS] + total[ROWS : 2 * ROWS] + total[:ROWS]) / divisor
        for r in range(ROUNDS):
            span = 2 * PAIRS
            start = pl.multiple_of(block * span, span)
            out_ref[r, pl.ds(start, span), :] = result[r * span : (r + 1) * span]
        return carry

    lax.fori_loop(0, blocks, finish, 0)

    def gather_sent(step, carry):
        gather_copy(step, peer(step)[0], flat).wait_send()
        return carry

    lax.fori_loop(1, group, gather_sent, 0)


def per_device(slc, map_cell):
    acq_count = lax.axis_size("acq")
    rng_count = lax.axis_size("rng")
    group = acq_count * rng_count
    lines, cols = slc.shape[2:]
    tile_lines = 2 * LOOK_A
    halves = BLOCK * tile_lines // lines
    tile_cols = cols // halves
    lanes = 2 * tile_cols // LOOK_R
    wide = 2 * rng_count * cols // LOOK_R
    radar = map_cell.shape[0] * map_cell.shape[1] * rng_count
    piece = MAPC // group
    pairs = acq_count // 2
    dma = pltpu.SemaphoreType.DMA
    result = pl.pallas_call(
        functools.partial(kernel, acq_count, rng_count),
        out_shape=jax.ShapeDtypeStruct((ROUNDS, pairs * 2, piece), F32),
        in_specs=[
            pl.BlockSpec(memory_space=pl.ANY),
            pl.BlockSpec(memory_space=pltpu.VMEM),
        ],
        out_specs=pl.BlockSpec(memory_space=pltpu.VMEM),
        scratch_shapes=[
            pltpu.VMEM((BLOCK, 2, tile_lines, tile_cols), BF16),
            pltpu.VMEM((rng_count,) + map_cell.shape, jnp.int32),
            pltpu.VMEM((group, ROWS, lanes), F32),
            pltpu.VMEM((piece, radar), BF16),
            pltpu.VMEM((tile_cols, lanes), BF16),
            pltpu.VMEM((wide, wide), BF16),
            dma,
            dma((BLOCK,)),
            dma((BLOCK,)),
            dma,
            dma,
            dma((group,)),
            dma((group,)),
        ],
        compiler_params=pltpu.CompilerParams(
            collective_id=0, has_side_effects=True, vmem_limit_bytes=40 * 2**20
        ),
    )(slc, map_cell)
    return result.reshape(ROUNDS, pairs, 2, piece)


def solution(mesh):
    in_specs = (P(None, ("groups", "acq"), None, "rng"), P("groups", "rng"))
    out_specs = P(None, "groups", None, ("acq", "rng"))
    return jax.shard_map(
        per_device, mesh=mesh, in_specs=in_specs, out_specs=out_specs, check_vma=False
    )
```

```python
import functools

import jax
import jax.numpy as jnp
from jax import lax
from jax.experimental import pallas as pl
from jax.experimental.pallas import tpu as pltpu
from jax.sharding import PartitionSpec as P

LOOK_A = 8
LOOK_R = 8
HALF_W = 4
ROUNDS = 3
MAPC = 16384
BLOCK = 2**ROUNDS
PAIRS = BLOCK // 2
SPAN = 2 * PAIRS
ROWS = ROUNDS * SPAN
HALF_PAIRS = ((0, 1), (2, 3), (0, 2), (1, 3))
MESH = pl.DeviceIdType.MESH
F32 = jnp.float32
BF16 = jnp.bfloat16


def split(value, terms):
    parts = []
    for _ in range(terms - 1):
        parts.append(value.astype(BF16).astype(F32))
        value = value - parts[-1]
    return [*parts, value]


def pair_products(low, up):
    real = low[0] * up[0] + low[1] * up[1]
    imag = low[1] * up[0] - low[0] * up[1]
    return [real, imag]


def power_product(sample):
    return [sample[0] * sample[0] + sample[1] * sample[1]]


def iota(shape, dim):
    return lax.broadcasted_iota(jnp.int32, shape, dim)


def kernel(
    acq_count,
    rng_count,
    slc_ref,
    map_ref,
    out_ref,
    samples,
    cells,
    gathered,
    one_hot,
    looks,
    band,
    own_sem,
    send_sem,
    recv_sem,
    map_send,
    map_recv,
    gather_send,
    gather_recv,
):
    group = acq_count * rng_count
    blocks = acq_count // BLOCK
    acq_rank = lax.axis_index("acq")
    rng_rank = lax.axis_index("rng")
    flat = acq_rank * rng_count + rng_rank
    base = acq_rank // BLOCK * BLOCK
    member = acq_rank % BLOCK
    tile_lines, tile_cols = samples.shape[2:]
    halves = slc_ref.shape[3] // tile_cols
    piece = out_ref.shape[2]

    def peer(far, core):
        other = acq_rank + far
        other = jnp.where(other >= acq_count, other - acq_count, other)
        side = rng_rank + core
        side = jnp.where(side >= rng_count, side - rng_count, side)
        return {"acq": other, "rng": side}, other * rng_count + side

    def for_peers(body):
        for core in range(1, rng_count):
            body(0, core)
        if acq_count <= 2 * BLOCK:
            for far in range(1, acq_count):
                for core in range(rng_count):
                    body(far, core)
            return

        def distant(far, carry):
            for core in range(rng_count):
                body(far, core)
            return carry

        lax.fori_loop(1, acq_count, distant, 0)

    barrier = pltpu.get_barrier_semaphore()

    def greet(far, core):
        pl.semaphore_signal(barrier, inc=1, device_id=peer(far, core)[0], device_id_type=MESH)

    for_peers(greet)
    pl.semaphore_wait(barrier, group - 1)

    def tile_of(target):
        line = pl.multiple_of(target // halves * tile_lines, tile_lines)
        col = pl.multiple_of(target % halves * tile_cols, tile_cols)
        return slc_ref.at[:, 0, pl.ds(line, tile_lines), pl.ds(col, tile_cols)]

    near = member // PAIRS * PAIRS
    distant = PAIRS - near
    sends = []
    for step in (4, 5, 6, 7, 1, 2, 3):
        target = (near if step < PAIRS else distant) + (member + step) % PAIRS
        copy = pltpu.make_async_remote_copy(
            src_ref=tile_of(target),
            dst_ref=samples.at[member],
            send_sem=send_sem.at[step],
            recv_sem=recv_sem.at[member],
            device_id={"acq": base + target},
            device_id_type=MESH,
        )
        copy.start()
        sends.append(copy)
    own = pltpu.make_async_copy(tile_of(member), samples.at[member], own_sem)
    own.start()
    map_copy = pltpu.make_async_remote_copy(
        src_ref=map_ref,
        dst_ref=cells.at[rng_rank],
        send_sem=map_send,
        recv_sem=map_recv,
        device_id={"rng": 1 - rng_rank},
        device_id_type=MESH,
    )
    map_copy.start()
    cells[rng_rank] = map_ref[...]

    look_cells = tile_cols // LOOK_R
    lanes = looks.shape[1]
    looks[...] = jnp.where(
        iota(looks.shape, 0) // LOOK_R == iota(looks.shape, 1) % look_cells, 1.0, 0.0
    ).astype(BF16)
    source = iota(band.shape, 0)
    target = iota(band.shape, 1)
    wide = rng_count * halves * look_cells
    source_cell = source // lanes * look_cells + source % look_cells
    source_look = source % lanes // look_cells
    gap = jnp.abs(source_cell - target % wide)
    weight = jnp.where(source_look == target // wide, jnp.maximum(HALF_W + 1 - gap, 0), 0)
    band[...] = weight.astype(F32).astype(BF16)

    map_copy.wait()
    columns = cells[...].reshape(rng_count * map_ref.shape[0], lanes).astype(F32).T
    place = iota((lanes, piece), 1).astype(F32) + (flat * piece).astype(F32)
    for line in range(map_ref.shape[0]):
        for core in range(rng_count):
            row = core * map_ref.shape[0] + line
            one_hot[pl.ds((line * rng_count + core) * lanes, lanes), :] = jnp.where(
                place == columns[:, row : row + 1], 1.0, 0.0
            ).astype(BF16)

    own.wait()
    look_weights = looks[...]
    lane = iota((1, 1, lanes), 2)

    def sample_arrival(origin):
        return pltpu.make_async_remote_copy(
            src_ref=samples.at[origin],
            dst_ref=samples.at[origin],
            send_sem=send_sem.at[0],
            recv_sem=recv_sem.at[origin],
            device_id={"acq": base + origin},
            device_id_type=MESH,
        )

    def load(origin):
        return samples[origin, 0].astype(F32), samples[origin, 1].astype(F32)

    def look_sums(products):
        stacked = jnp.concatenate(products, axis=0)
        summed = sum(
            jnp.dot(part.astype(BF16), look_weights, preferred_element_type=F32)
            for part in reversed(split(stacked, 3))
        )
        summed = summed.reshape(len(products), tile_lines, lanes)
        chosen = jnp.where(lane < look_cells, summed[:, :LOOK_A], summed[:, LOOK_A:])
        return jnp.sum(chosen, axis=1)

    def coherence(sums, power_low, power_up):
        low = jnp.concatenate([p for p in power_low for _ in range(2)], axis=0)
        up = jnp.concatenate([p for p in power_up for _ in range(2)], axis=0)
        return sums * (1.0 / jnp.sqrt(low * up + 1e-06))

    def half_products(four):
        products = []
        for low, up in HALF_PAIRS:
            products += pair_products(four[low], four[up])
        for sample in four:
            products += power_product(sample)
        return products

    def half_coherence(sums):
        power = [sums[SPAN + a : SPAN + a + 1] for a in range(PAIRS)]
        gamma = coherence(
            sums[:SPAN], [power[low] for low, _ in HALF_PAIRS], [power[up] for _, up in HALF_PAIRS]
        )
        return gamma, power

    def gather_copy(far, core, late, arriving):
        index, other = peer(far, core)
        slot = other if arriving else flat
        rows = pl.ds(SPAN, ROWS - SPAN) if late else pl.ds(0, SPAN)
        return pltpu.make_async_remote_copy(
            src_ref=gathered.at[slot, rows],
            dst_ref=gathered.at[slot, rows],
            send_sem=gather_send.at[late, far * rng_count + core],
            recv_sem=gather_recv.at[late, slot],
            device_id=index,
            device_id_type=MESH,
        )

    for step in range(1, PAIRS):
        sample_arrival(near + (member + step) % PAIRS).wait_recv()
    near_sums = look_sums(half_products([load(near + a) for a in range(PAIRS)]))
    gathered[flat, :SPAN], near_power = half_coherence(near_sums)
    for_peers(lambda far, core: gather_copy(far, core, 0, False).start())

    for step in range(PAIRS):
        sample_arrival(distant + (member + step) % PAIRS).wait_recv()
    products = half_products([load(distant + a) for a in range(PAIRS)])
    for a in range(PAIRS):
        products += pair_products(load(a), load(PAIRS + a))
    late_sums = look_sums(products)
    half_rows = SPAN + PAIRS
    far_gamma, far_power = half_coherence(late_sums[:half_rows])
    gathered[flat, SPAN:] = jnp.concatenate(
        [far_gamma, coherence(late_sums[half_rows:], near_power, far_power)], axis=0
    )
    for_peers(lambda far, core: gather_copy(far, core, 1, False).start())
    for copy in sends:
        copy.wait_send()
    for late in range(2):
        for_peers(lambda far, core: gather_copy(far, core, late, True).wait_recv())

    quarters = BLOCK // halves
    even = iota((quarters * ROWS, 1), 0) % 2 == 0
    ones = jnp.ones((8, quarters * band.shape[1]), F32)

    def piece_of(block, i, c):
        slot = (block * BLOCK + i) * rng_count + c
        if i < PAIRS:
            return gathered[slot]
        return jnp.concatenate(
            [gathered[slot, SPAN : 2 * SPAN], gathered[slot, :SPAN], gathered[slot, 2 * SPAN :]],
            axis=0,
        )

    def finish(block, carry):
        rows = []
        for q in range(quarters):
            parts = [
                piece_of(block, q * halves + h, c)
                for c in range(rng_count)
                for h in range(halves)
            ]
            rows.append(jnp.concatenate(parts, axis=1))
        gamma = jnp.concatenate(rows, axis=0)
        smooth = sum(
            jnp.dot(part.astype(BF16), band[...], preferred_element_type=F32)
            for part in reversed(split(gamma, 2))
        ) * (1.0 / (HALF_W + 1) ** 2)
        square = smooth * smooth
        count = square.shape[0]
        partner = jnp.where(even, pltpu.roll(square, count - 1, 0), pltpu.roll(square, 1, 0))
        filtered = smooth * lax.rsqrt(jnp.sqrt(square + partner + 0.01))
        flat_rows = jnp.concatenate(
            [filtered[q * ROWS : (q + 1) * ROWS] for q in range(quarters)], axis=1
        )
        left = jnp.concatenate([*split(flat_rows, 2), ones], axis=0).astype(BF16)
        total = jnp.dot(left, one_hot[...], preferred_element_type=F32)
        divisor = jnp.maximum(total[2 * ROWS : 2 * ROWS + 1], 1.0)
        result = (total[ROWS : 2 * ROWS] + total[:ROWS]) / divisor
        start = pl.multiple_of(block * SPAN, SPAN)
        low, high, cross = result[:SPAN], result[SPAN : 2 * SPAN], result[2 * SPAN :]
        for r in range(2):
            rows = slice(r * PAIRS, (r + 1) * PAIRS)
            both = jnp.concatenate([low[rows], high[rows]], axis=0)
            out_ref[r, pl.ds(start, SPAN), :] = both
        out_ref[2, pl.ds(start, SPAN), :] = cross
        return carry

    lax.fori_loop(0, blocks, finish, 0)

    for late in range(2):
        for_peers(lambda far, core: gather_copy(far, core, late, False).wait_send())


def per_device(slc, map_cell):
    acq_count = lax.axis_size("acq")
    rng_count = lax.axis_size("rng")
    group = acq_count * rng_count
    lines, cols = slc.shape[2:]
    tile_lines = 2 * LOOK_A
    halves = BLOCK * tile_lines // lines
    tile_cols = cols // halves
    lanes = 2 * tile_cols // LOOK_R
    wide = 2 * rng_count * cols // LOOK_R
    radar = map_cell.shape[0] * map_cell.shape[1] * rng_count
    piece = MAPC // group
    pairs = acq_count // 2
    dma = pltpu.SemaphoreType.DMA
    result = pl.pallas_call(
        functools.partial(kernel, acq_count, rng_count),
        out_shape=jax.ShapeDtypeStruct((ROUNDS, pairs * 2, piece), F32),
        in_specs=[
            pl.BlockSpec(memory_space=pl.ANY),
            pl.BlockSpec(memory_space=pltpu.VMEM),
        ],
        out_specs=pl.BlockSpec(memory_space=pltpu.VMEM),
        scratch_shapes=[
            pltpu.VMEM((BLOCK, 2, tile_lines, tile_cols), BF16),
            pltpu.VMEM((rng_count,) + map_cell.shape, jnp.int32),
            pltpu.VMEM((group, ROWS, lanes), F32),
            pltpu.VMEM((radar, piece), BF16),
            pltpu.VMEM((tile_cols, lanes), BF16),
            pltpu.VMEM((wide, wide), BF16),
            dma,
            dma((BLOCK,)),
            dma((BLOCK,)),
            dma,
            dma,
            dma((2, group)),
            dma((2, group)),
        ],
        compiler_params=pltpu.CompilerParams(
            collective_id=0, has_side_effects=True, vmem_limit_bytes=40 * 2**20
        ),
    )(slc, map_cell)
    return result.reshape(ROUNDS, pairs, 2, piece)


def solution(mesh):
    in_specs = (P(None, ("groups", "acq"), None, "rng"), P("groups", "rng"))
    out_specs = P(None, "groups", None, ("acq", "rng"))
    return jax.shard_map(
        per_device, mesh=mesh, in_specs=in_specs, out_specs=out_specs, check_vma=False
    )
```

```python
import functools

import jax
import jax.numpy as jnp
from jax import lax
from jax.experimental import pallas as pl
from jax.experimental.pallas import tpu as pltpu
from jax.sharding import PartitionSpec as P

LOOK_A = 8
LOOK_R = 8
HALF_W = 4
ROUNDS = 3
MAPC = 16384
BLOCK = 2**ROUNDS
PAIRS = BLOCK // 2
SPAN = 2 * PAIRS
ROWS = ROUNDS * SPAN
HALF_PAIRS = ((0, 1), (2, 3), (0, 2), (1, 3))
MESH = pl.DeviceIdType.MESH
F32 = jnp.float32
BF16 = jnp.bfloat16


def split(value, terms):
    parts = []
    for _ in range(terms - 1):
        parts.append(value.astype(BF16).astype(F32))
        value = value - parts[-1]
    return [*parts, value]


def pair_products(low, up):
    real = low[0] * up[0] + low[1] * up[1]
    imag = low[1] * up[0] - low[0] * up[1]
    return [real, imag]


def power_product(sample):
    return [sample[0] * sample[0] + sample[1] * sample[1]]


def iota(shape, dim):
    return lax.broadcasted_iota(jnp.int32, shape, dim)


def kernel(
    acq_count,
    rng_count,
    slc_ref,
    map_ref,
    out_ref,
    samples,
    cells,
    gathered,
    one_hot,
    looks,
    band,
    own_sem,
    send_sem,
    recv_sem,
    map_send,
    map_recv,
    gather_send,
    gather_recv,
):
    group = acq_count * rng_count
    blocks = acq_count // BLOCK
    acq_rank = lax.axis_index("acq")
    rng_rank = lax.axis_index("rng")
    flat = acq_rank * rng_count + rng_rank
    base = acq_rank // BLOCK * BLOCK
    member = acq_rank % BLOCK
    tile_lines, tile_cols = samples.shape[2:]
    halves = slc_ref.shape[3] // tile_cols
    piece = out_ref.shape[2]

    def peer(far, core):
        other = acq_rank + far
        other = jnp.where(other >= acq_count, other - acq_count, other)
        side = rng_rank + core
        side = jnp.where(side >= rng_count, side - rng_count, side)
        return {"acq": other, "rng": side}, other * rng_count + side

    def for_peers(body):
        for core in range(1, rng_count):
            body(0, core)
        if acq_count <= 2 * BLOCK:
            for far in range(1, acq_count):
                for core in range(rng_count):
                    body(far, core)
            return

        def distant(far, carry):
            for core in range(rng_count):
                body(far, core)
            return carry

        lax.fori_loop(1, acq_count, distant, 0)

    barrier = pltpu.get_barrier_semaphore()

    def greet(far, core):
        pl.semaphore_signal(barrier, inc=1, device_id=peer(far, core)[0], device_id_type=MESH)

    for_peers(greet)
    pl.semaphore_wait(barrier, group - 1)

    def tile_of(target):
        line = pl.multiple_of(target // halves * tile_lines, tile_lines)
        col = pl.multiple_of(target % halves * tile_cols, tile_cols)
        return slc_ref.at[:, 0, pl.ds(line, tile_lines), pl.ds(col, tile_cols)]

    near = member // PAIRS * PAIRS
    distant = PAIRS - near
    sends = []
    for step in (4, 5, 6, 7, 1, 2, 3):
        target = (near if step < PAIRS else distant) + (member + step) % PAIRS
        copy = pltpu.make_async_remote_copy(
            src_ref=tile_of(target),
            dst_ref=samples.at[member],
            send_sem=send_sem.at[step],
            recv_sem=recv_sem.at[member],
            device_id={"acq": base + target},
            device_id_type=MESH,
        )
        copy.start()
        sends.append(copy)
    own = pltpu.make_async_copy(tile_of(member), samples.at[member], own_sem)
    own.start()
    map_copy = pltpu.make_async_remote_copy(
        src_ref=map_ref,
        dst_ref=cells.at[rng_rank],
        send_sem=map_send,
        recv_sem=map_recv,
        device_id={"rng": 1 - rng_rank},
        device_id_type=MESH,
    )
    map_copy.start()
    cells[rng_rank] = map_ref[...]

    look_cells = tile_cols // LOOK_R
    lanes = looks.shape[1]
    looks[...] = jnp.where(
        iota(looks.shape, 0) // LOOK_R == iota(looks.shape, 1) % look_cells, 1.0, 0.0
    ).astype(BF16)
    source = iota(band.shape, 0)
    target = iota(band.shape, 1)
    wide = rng_count * halves * look_cells
    source_cell = source // lanes * look_cells + source % look_cells
    source_look = source % lanes // look_cells
    gap = jnp.abs(source_cell - target % wide)
    weight = jnp.where(source_look == target // wide, jnp.maximum(HALF_W + 1 - gap, 0), 0)
    band[...] = weight.astype(F32).astype(BF16)

    map_copy.wait()
    columns = cells[...].reshape(rng_count * map_ref.shape[0], lanes).astype(F32).T
    place = iota((lanes, piece), 1).astype(F32) + (flat * piece).astype(F32)
    for line in range(map_ref.shape[0]):
        for core in range(rng_count):
            row = core * map_ref.shape[0] + line
            one_hot[pl.ds((line * rng_count + core) * lanes, lanes), :] = jnp.where(
                place == columns[:, row : row + 1], 1.0, 0.0
            ).astype(BF16)

    own.wait()
    look_weights = looks[...]
    lane = iota((1, 1, lanes), 2)

    def sample_arrival(origin):
        return pltpu.make_async_remote_copy(
            src_ref=samples.at[origin],
            dst_ref=samples.at[origin],
            send_sem=send_sem.at[0],
            recv_sem=recv_sem.at[origin],
            device_id={"acq": base + origin},
            device_id_type=MESH,
        )

    def load(origin):
        return samples[origin, 0].astype(F32), samples[origin, 1].astype(F32)

    def look_sums(products):
        stacked = jnp.concatenate(products, axis=0)
        summed = sum(
            jnp.dot(part.astype(BF16), look_weights, preferred_element_type=F32)
            for part in reversed(split(stacked, 3))
        )
        summed = summed.reshape(len(products), tile_lines, lanes)
        chosen = jnp.where(lane < look_cells, summed[:, :LOOK_A], summed[:, LOOK_A:])
        return jnp.sum(chosen, axis=1)

    def coherence(sums, power_low, power_up):
        low = jnp.concatenate([p for p in power_low for _ in range(2)], axis=0)
        up = jnp.concatenate([p for p in power_up for _ in range(2)], axis=0)
        return sums * (1.0 / jnp.sqrt(low * up + 1e-06))

    def half_products(four):
        products = []
        for low, up in HALF_PAIRS:
            products += pair_products(four[low], four[up])
        for sample in four:
            products += power_product(sample)
        return products

    def half_coherence(sums):
        power = [sums[SPAN + a : SPAN + a + 1] for a in range(PAIRS)]
        gamma = coherence(
            sums[:SPAN], [power[low] for low, _ in HALF_PAIRS], [power[up] for _, up in HALF_PAIRS]
        )
        return gamma, power

    def gather_copy(far, core, late, arriving):
        index, other = peer(far, core)
        slot = other if arriving else flat
        rows = pl.ds(SPAN, ROWS - SPAN) if late else pl.ds(0, SPAN)
        return pltpu.make_async_remote_copy(
            src_ref=gathered.at[slot, rows],
            dst_ref=gathered.at[slot, rows],
            send_sem=gather_send.at[late, far * rng_count + core],
            recv_sem=gather_recv.at[late, slot],
            device_id=index,
            device_id_type=MESH,
        )

    for step in range(1, PAIRS):
        sample_arrival(near + (member + step) % PAIRS).wait_recv()
    near_sums = look_sums(half_products([load(near + a) for a in range(PAIRS)]))
    gathered[flat, :SPAN], near_power = half_coherence(near_sums)
    for_peers(lambda far, core: gather_copy(far, core, 0, False).start())

    for step in range(PAIRS):
        sample_arrival(distant + (member + step) % PAIRS).wait_recv()
    products = half_products([load(distant + a) for a in range(PAIRS)])
    for a in range(PAIRS):
        products += pair_products(load(a), load(PAIRS + a))
    late_sums = look_sums(products)
    half_rows = SPAN + PAIRS
    far_gamma, far_power = half_coherence(late_sums[:half_rows])
    gathered[flat, SPAN:] = jnp.concatenate(
        [far_gamma, coherence(late_sums[half_rows:], near_power, far_power)], axis=0
    )
    for_peers(lambda far, core: gather_copy(far, core, 1, False).start())
    for copy in sends:
        copy.wait_send()
    for late in range(2):
        for_peers(lambda far, core: gather_copy(far, core, late, True).wait_recv())

    quarters = BLOCK // halves
    even = iota((quarters * ROWS, 1), 0) % 2 == 0
    ones = jnp.ones((8, quarters * band.shape[1]), F32)

    def piece_of(block, i, c):
        slot = (block * BLOCK + i) * rng_count + c
        if i < PAIRS:
            return gathered[slot]
        return jnp.concatenate(
            [gathered[slot, SPAN : 2 * SPAN], gathered[slot, :SPAN], gathered[slot, 2 * SPAN :]],
            axis=0,
        )

    def finish(block, carry):
        rows = []
        for q in range(quarters):
            parts = [
                piece_of(block, q * halves + h, c)
                for c in range(rng_count)
                for h in range(halves)
            ]
            rows.append(jnp.concatenate(parts, axis=1))
        gamma = jnp.concatenate(rows, axis=0)
        smooth = sum(
            jnp.dot(part.astype(BF16), band[...], preferred_element_type=F32)
            for part in reversed(split(gamma, 2))
        ) * (1.0 / (HALF_W + 1) ** 2)
        square = smooth * smooth
        count = square.shape[0]
        partner = jnp.where(even, pltpu.roll(square, count - 1, 0), pltpu.roll(square, 1, 0))
        filtered = smooth * lax.rsqrt(jnp.sqrt(square + partner + 0.01))
        flat_rows = jnp.concatenate(
            [filtered[q * ROWS : (q + 1) * ROWS] for q in range(quarters)], axis=1
        )
        left = jnp.concatenate([*split(flat_rows, 2), ones], axis=0).astype(BF16)
        total = jnp.dot(left, one_hot[...], preferred_element_type=F32)
        divisor = jnp.maximum(total[2 * ROWS : 2 * ROWS + 1], 1.0)
        result = (total[ROWS : 2 * ROWS] + total[:ROWS]) / divisor
        start = pl.multiple_of(block * SPAN, SPAN)
        low, high, cross = result[:SPAN], result[SPAN : 2 * SPAN], result[2 * SPAN :]
        for r in range(2):
            rows = slice(r * PAIRS, (r + 1) * PAIRS)
            both = jnp.concatenate([low[rows], high[rows]], axis=0)
            out_ref[r, pl.ds(start, SPAN), :] = both
        out_ref[2, pl.ds(start, SPAN), :] = cross
        return carry

    lax.fori_loop(0, blocks, finish, 0)

    for late in range(2):
        for_peers(lambda far, core: gather_copy(far, core, late, False).wait_send())


def per_device(slc, map_cell):
    acq_count = lax.axis_size("acq")
    rng_count = lax.axis_size("rng")
    group = acq_count * rng_count
    lines, cols = slc.shape[2:]
    tile_lines = 2 * LOOK_A
    halves = BLOCK * tile_lines // lines
    tile_cols = cols // halves
    lanes = 2 * tile_cols // LOOK_R
    wide = 2 * rng_count * cols // LOOK_R
    radar = map_cell.shape[0] * map_cell.shape[1] * rng_count
    piece = MAPC // group
    pairs = acq_count // 2
    dma = pltpu.SemaphoreType.DMA
    result = pl.pallas_call(
        functools.partial(kernel, acq_count, rng_count),
        out_shape=jax.ShapeDtypeStruct((ROUNDS, pairs * 2, piece), F32),
        in_specs=[
            pl.BlockSpec(memory_space=pl.ANY),
            pl.BlockSpec(memory_space=pltpu.VMEM),
        ],
        out_specs=pl.BlockSpec(memory_space=pltpu.VMEM),
        scratch_shapes=[
            pltpu.VMEM((BLOCK, 2, tile_lines, tile_cols), BF16),
            pltpu.VMEM((rng_count,) + map_cell.shape, jnp.int32),
            pltpu.VMEM((group, ROWS, lanes), F32),
            pltpu.VMEM((radar, piece), BF16),
            pltpu.VMEM((tile_cols, lanes), BF16),
            pltpu.VMEM((wide, wide), BF16),
            dma,
            dma((BLOCK,)),
            dma((BLOCK,)),
            dma,
            dma,
            dma((2, group)),
            dma((2, group)),
        ],
        compiler_params=pltpu.CompilerParams(
            collective_id=0, has_side_effects=True, vmem_limit_bytes=int(53.72 * 2**20)
        ),
    )(slc, map_cell)
    return result.reshape(ROUNDS, pairs, 2, piece)


def solution(mesh):
    in_specs = (P(None, ("groups", "acq"), None, "rng"), P("groups", "rng"))
    out_specs = P(None, "groups", None, ("acq", "rng"))
    return jax.shard_map(
        per_device, mesh=mesh, in_specs=in_specs, out_specs=out_specs, check_vma=False
    )
```

```python
import functools

import jax
import jax.numpy as jnp
from jax import lax
from jax.experimental import pallas as pl
from jax.experimental.pallas import tpu as pltpu
from jax.sharding import PartitionSpec as P

LOOK_A = 8
LOOK_R = 8
HALF_W = 4
ROUNDS = 3
MAPC = 16384
BLOCK = 2**ROUNDS
PAIRS = BLOCK // 2
SPAN = 2 * PAIRS
ROWS = ROUNDS * SPAN
HALF_PAIRS = ((0, 1), (2, 3), (0, 2), (1, 3))
MESH = pl.DeviceIdType.MESH
F32 = jnp.float32
BF16 = jnp.bfloat16


def split(value, terms):
    parts = []
    for _ in range(terms - 1):
        parts.append(value.astype(BF16).astype(F32))
        value = value - parts[-1]
    return [*parts, value]


def pair_products(low, up):
    real = low[0] * up[0] + low[1] * up[1]
    imag = low[1] * up[0] - low[0] * up[1]
    return [real, imag]


def power_product(sample):
    return [sample[0] * sample[0] + sample[1] * sample[1]]


def iota(shape, dim):
    return lax.broadcasted_iota(jnp.int32, shape, dim)


def kernel(
    acq_count,
    rng_count,
    slc_ref,
    map_ref,
    out_ref,
    samples,
    cells,
    gathered,
    one_hot,
    looks,
    band,
    own_sem,
    send_sem,
    recv_sem,
    map_send,
    map_recv,
    gather_send,
    gather_recv,
):
    group = acq_count * rng_count
    blocks = acq_count // BLOCK
    acq_rank = lax.axis_index("acq")
    rng_rank = lax.axis_index("rng")
    flat = acq_rank * rng_count + rng_rank
    base = acq_rank // BLOCK * BLOCK
    member = acq_rank % BLOCK
    tile_lines, tile_cols = samples.shape[2:]
    halves = slc_ref.shape[3] // tile_cols
    piece = out_ref.shape[2]

    def peer(far, core):
        other = acq_rank + far
        other = jnp.where(other >= acq_count, other - acq_count, other)
        side = rng_rank + core
        side = jnp.where(side >= rng_count, side - rng_count, side)
        return {"acq": other, "rng": side}, other * rng_count + side

    def for_peers(body):
        for core in range(1, rng_count):
            body(0, core)
        if acq_count <= 2 * BLOCK:
            for far in range(1, acq_count):
                body(far, 0)
            for core in range(1, rng_count):
                for far in range(1, acq_count):
                    body(far, core)
            return

        def distant(far, carry):
            for core in range(rng_count):
                body(far, core)
            return carry

        lax.fori_loop(1, acq_count, distant, 0)

    barrier = pltpu.get_barrier_semaphore()

    def greet(far, core):
        pl.semaphore_signal(barrier, inc=1, device_id=peer(far, core)[0], device_id_type=MESH)

    for_peers(greet)
    pl.semaphore_wait(barrier, group - 1)

    def tile_of(target):
        line = pl.multiple_of(target // halves * tile_lines, tile_lines)
        col = pl.multiple_of(target % halves * tile_cols, tile_cols)
        return slc_ref.at[:, 0, pl.ds(line, tile_lines), pl.ds(col, tile_cols)]

    near = member // PAIRS * PAIRS
    distant = PAIRS - near
    sends = []
    for step in (4, 5, 6, 7, 1, 2, 3):
        target = (near if step < PAIRS else distant) + (member + step) % PAIRS
        copy = pltpu.make_async_remote_copy(
            src_ref=tile_of(target),
            dst_ref=samples.at[member],
            send_sem=send_sem.at[step],
            recv_sem=recv_sem.at[member],
            device_id={"acq": base + target},
            device_id_type=MESH,
        )
        copy.start()
        sends.append(copy)
    own = pltpu.make_async_copy(tile_of(member), samples.at[member], own_sem)
    own.start()
    map_copy = pltpu.make_async_remote_copy(
        src_ref=map_ref,
        dst_ref=cells.at[rng_rank],
        send_sem=map_send,
        recv_sem=map_recv,
        device_id={"rng": 1 - rng_rank},
        device_id_type=MESH,
    )
    map_copy.start()
    cells[rng_rank] = map_ref[...]

    look_cells = tile_cols // LOOK_R
    lanes = looks.shape[1]
    looks[...] = jnp.where(
        iota(looks.shape, 0) // LOOK_R == iota(looks.shape, 1) % look_cells, 1.0, 0.0
    ).astype(BF16)
    source = iota(band.shape, 0)
    target = iota(band.shape, 1)
    wide = rng_count * halves * look_cells
    source_cell = source // lanes * look_cells + source % look_cells
    source_look = source % lanes // look_cells
    gap = jnp.abs(source_cell - target % wide)
    weight = jnp.where(source_look == target // wide, jnp.maximum(HALF_W + 1 - gap, 0), 0)
    band[...] = weight.astype(F32).astype(BF16)

    map_copy.wait()
    columns = cells[...].reshape(rng_count * map_ref.shape[0], lanes).astype(F32).T
    place = iota((lanes, piece), 1).astype(F32) + (flat * piece).astype(F32)
    for line in range(map_ref.shape[0]):
        for core in range(rng_count):
            row = core * map_ref.shape[0] + line
            one_hot[pl.ds((line * rng_count + core) * lanes, lanes), :] = jnp.where(
                place == columns[:, row : row + 1], 1.0, 0.0
            ).astype(BF16)

    own.wait()
    look_weights = looks[...]
    lane = iota((1, 1, lanes), 2)

    def sample_arrival(origin):
        return pltpu.make_async_remote_copy(
            src_ref=samples.at[origin],
            dst_ref=samples.at[origin],
            send_sem=send_sem.at[0],
            recv_sem=recv_sem.at[origin],
            device_id={"acq": base + origin},
            device_id_type=MESH,
        )

    def load(origin):
        return samples[origin, 0].astype(F32), samples[origin, 1].astype(F32)

    def look_sums(products):
        stacked = jnp.concatenate(products, axis=0)
        summed = sum(
            jnp.dot(part.astype(BF16), look_weights, preferred_element_type=F32)
            for part in reversed(split(stacked, 3))
        )
        summed = summed.reshape(len(products), tile_lines, lanes)
        chosen = jnp.where(lane < look_cells, summed[:, :LOOK_A], summed[:, LOOK_A:])
        return jnp.sum(chosen, axis=1)

    def coherence(sums, power_low, power_up):
        low = jnp.concatenate([p for p in power_low for _ in range(2)], axis=0)
        up = jnp.concatenate([p for p in power_up for _ in range(2)], axis=0)
        return sums * (1.0 / jnp.sqrt(low * up + 1e-06))

    def half_products(four):
        products = []
        for low, up in HALF_PAIRS:
            products += pair_products(four[low], four[up])
        for sample in four:
            products += power_product(sample)
        return products

    def half_coherence(sums):
        power = [sums[SPAN + a : SPAN + a + 1] for a in range(PAIRS)]
        gamma = coherence(
            sums[:SPAN], [power[low] for low, _ in HALF_PAIRS], [power[up] for _, up in HALF_PAIRS]
        )
        return gamma, power

    def gather_copy(far, core, late, arriving):
        index, other = peer(far, core)
        slot = other if arriving else flat
        rows = pl.ds(SPAN, ROWS - SPAN) if late else pl.ds(0, SPAN)
        return pltpu.make_async_remote_copy(
            src_ref=gathered.at[slot, rows],
            dst_ref=gathered.at[slot, rows],
            send_sem=gather_send.at[late, far * rng_count + core],
            recv_sem=gather_recv.at[late, slot],
            device_id=index,
            device_id_type=MESH,
        )

    for step in range(1, PAIRS):
        sample_arrival(near + (member + step) % PAIRS).wait_recv()
    near_sums = look_sums(half_products([load(near + a) for a in range(PAIRS)]))
    gathered[flat, :SPAN], near_power = half_coherence(near_sums)
    for_peers(lambda far, core: gather_copy(far, core, 0, False).start())

    for step in range(PAIRS):
        sample_arrival(distant + (member + step) % PAIRS).wait_recv()
    products = half_products([load(distant + a) for a in range(PAIRS)])
    for a in range(PAIRS):
        products += pair_products(load(a), load(PAIRS + a))
    late_sums = look_sums(products)
    half_rows = SPAN + PAIRS
    far_gamma, far_power = half_coherence(late_sums[:half_rows])
    gathered[flat, SPAN:] = jnp.concatenate(
        [far_gamma, coherence(late_sums[half_rows:], near_power, far_power)], axis=0
    )
    for_peers(lambda far, core: gather_copy(far, core, 1, False).start())
    for copy in sends:
        copy.wait_send()
    for late in range(2):
        for_peers(lambda far, core: gather_copy(far, core, late, True).wait_recv())

    quarters = BLOCK // halves
    even = iota((quarters * ROWS, 1), 0) % 2 == 0
    ones = jnp.ones((8, quarters * band.shape[1]), F32)

    def piece_of(block, i, c):
        slot = (block * BLOCK + i) * rng_count + c
        if i < PAIRS:
            return gathered[slot]
        return jnp.concatenate(
            [gathered[slot, SPAN : 2 * SPAN], gathered[slot, :SPAN], gathered[slot, 2 * SPAN :]],
            axis=0,
        )

    def finish(block, carry):
        rows = []
        for q in range(quarters):
            parts = [
                piece_of(block, q * halves + h, c)
                for c in range(rng_count)
                for h in range(halves)
            ]
            rows.append(jnp.concatenate(parts, axis=1))
        gamma = jnp.concatenate(rows, axis=0)
        smooth = sum(
            jnp.dot(part.astype(BF16), band[...], preferred_element_type=F32)
            for part in reversed(split(gamma, 2))
        ) * (1.0 / (HALF_W + 1) ** 2)
        square = smooth * smooth
        count = square.shape[0]
        partner = jnp.where(even, pltpu.roll(square, count - 1, 0), pltpu.roll(square, 1, 0))
        filtered = smooth * lax.rsqrt(jnp.sqrt(square + partner + 0.01))
        flat_rows = jnp.concatenate(
            [filtered[q * ROWS : (q + 1) * ROWS] for q in range(quarters)], axis=1
        )
        left = jnp.concatenate([*split(flat_rows, 2), ones], axis=0).astype(BF16)
        total = jnp.dot(left, one_hot[...], preferred_element_type=F32)
        divisor = jnp.maximum(total[2 * ROWS : 2 * ROWS + 1], 1.0)
        result = (total[ROWS : 2 * ROWS] + total[:ROWS]) / divisor
        start = pl.multiple_of(block * SPAN, SPAN)
        low, high, cross = result[:SPAN], result[SPAN : 2 * SPAN], result[2 * SPAN :]
        for r in range(2):
            rows = slice(r * PAIRS, (r + 1) * PAIRS)
            both = jnp.concatenate([low[rows], high[rows]], axis=0)
            out_ref[r, pl.ds(start, SPAN), :] = both
        out_ref[2, pl.ds(start, SPAN), :] = cross
        return carry

    lax.fori_loop(0, blocks, finish, 0)

    for late in range(2):
        for_peers(lambda far, core: gather_copy(far, core, late, False).wait_send())


def per_device(slc, map_cell):
    acq_count = lax.axis_size("acq")
    rng_count = lax.axis_size("rng")
    group = acq_count * rng_count
    lines, cols = slc.shape[2:]
    tile_lines = 2 * LOOK_A
    halves = BLOCK * tile_lines // lines
    tile_cols = cols // halves
    lanes = 2 * tile_cols // LOOK_R
    wide = 2 * rng_count * cols // LOOK_R
    radar = map_cell.shape[0] * map_cell.shape[1] * rng_count
    piece = MAPC // group
    pairs = acq_count // 2
    dma = pltpu.SemaphoreType.DMA
    result = pl.pallas_call(
        functools.partial(kernel, acq_count, rng_count),
        out_shape=jax.ShapeDtypeStruct((ROUNDS, pairs * 2, piece), F32),
        in_specs=[
            pl.BlockSpec(memory_space=pl.ANY),
            pl.BlockSpec(memory_space=pltpu.VMEM),
        ],
        out_specs=pl.BlockSpec(memory_space=pltpu.VMEM),
        scratch_shapes=[
            pltpu.VMEM((BLOCK, 2, tile_lines, tile_cols), BF16),
            pltpu.VMEM((rng_count,) + map_cell.shape, jnp.int32),
            pltpu.VMEM((group, ROWS, lanes), F32),
            pltpu.VMEM((radar, piece), BF16),
            pltpu.VMEM((tile_cols, lanes), BF16),
            pltpu.VMEM((wide, wide), BF16),
            dma,
            dma((BLOCK,)),
            dma((BLOCK,)),
            dma,
            dma,
            dma((2, group)),
            dma((2, group)),
        ],
        compiler_params=pltpu.CompilerParams(
            collective_id=0, has_side_effects=True, vmem_limit_bytes=int(53.72 * 2**20)
        ),
    )(slc, map_cell)
    return result.reshape(ROUNDS, pairs, 2, piece)


def solution(mesh):
    in_specs = (P(None, ("groups", "acq"), None, "rng"), P("groups", "rng"))
    out_specs = P(None, "groups", None, ("acq", "rng"))
    return jax.shard_map(
        per_device, mesh=mesh, in_specs=in_specs, out_specs=out_specs, check_vma=False
    )
```
